32 devices in a mesh: expert: 16 (over z, x, core), dp: 2 (over y).
Axes of the slice: x: 2, y: 2, z: 4, core: 2. Of those that a mesh axis runs over, the one named last changes fastest.
Arguments:
- skip_stream: bfloat16 [256, 4096], P(('expert', 'dp')), may hold values from -6 to 6
- attention_probes: bfloat16 [256, 4096], P(('expert', 'dp')), may hold values from -5 to 5
- stored_attention_lookups: bfloat16 [256, 16, 512], P(('expert', 'dp')), may hold values from -5 to 5
- stored_attention_contents: bfloat16 [256, 16, 512], P(('expert', 'dp')), may hold values from -6 to 6
- incoming_lookup_entries: bfloat16 [256, 512], P(('expert', 'dp')), may hold values from -6 to 6
- incoming_content_entries: bfloat16 [256, 512], P(('expert', 'dp')), may hold values from -6 to 6
- filled_slot_spans: int32 [256], P(('expert', 'dp')), may hold values from 2 to 16, as said below
- layernorm_gain: float32 [4096], replicated, may hold values from 0.1 to 1.9
- routed_specialist_indices: int32 [256, 8], P(('expert', 'dp')), may hold values from 0 to 15, all different within a row; in each aligned block of 8 rows (0 to 7, 8 to 15, ...) at most 4 rows name the same one
- routing_probabilities: float32 [256, 8], P(('expert', 'dp')), may hold values from 0.05 to 1
- admission_limits: int32 [16], replicated, may hold values from 64 to 256
- swap_indicator: int32 [16], replicated, may hold values from 0 to 1, as said below
- gating_projection_matrix: bfloat16 [16, 768, 4096], P('expert', 'dp'), may hold values from -0.09375 to 0.09375
- widening_projection_matrix: bfloat16 [16, 768, 4096], P('expert', 'dp'), may hold values from -0.09375 to 0.09375
- output_projection_matrix: bfloat16 [16, 768, 4096], P('expert', None, 'dp'), may hold values from -0.21875 to 0.21875
Outputs:
- layer_out: bfloat16 [256, 4096], P(('expert', 'dp'))
- device_share: float32 [16], P('expert')
- held_gate: bfloat16 [16, 768, 4096], P('expert', 'dp')
- held_up: bfloat16 [16, 768, 4096], P('expert', 'dp')
- held_down: bfloat16 [16, 768, 4096], P('expert', None, 'dp')
The draws below stay inside these ranges and needn't reach their ends.
Inputs may be any that keep to these rules, and one draw needn't show every extreme that they name: `filled_slot_spans`: each sequence has 2 or more valid slots and some sequence has all 16. `routed_specialist_indices`: in each aligned block of 8 rows (the rows of one device) no expert is named by more than 4 rows; the entries of a row differ. swap_indicator[i] equals swap_indicator[i + 8].
All inputs are finite; a program needn't handle non-finite values.
Results may differ from the reference program's by a relative error of at most 0.017.
Values may be sent and summed in bfloat16 or wider, within the bound.
A program may use at most 64 MiB of HBM per device.

```python
import math
import jax
import jax.numpy as jnp
import numpy as np
from jax import lax

D = 4096
QH = 32
KVH = 4
HEAD = 128
EXPERT_FF = 768
ROUTED_PER_TOKEN = 8
LEN = 16
LOCAL_STREAMS = 8
SPECIALIST_NUM = 16
CAP = 4
GLOBAL_STREAMS = 256
DEVICES = 32


def drawn_fields(key):
    query_key = jax.random.fold_in(key, 11)
    cache_key = jax.random.fold_in(key, 12)
    query_part = jnp.clip(jax.random.normal(query_key, (GLOBAL_STREAMS, QH * HEAD), jnp.float32), -5.0, 5.0)
    cache_part = jnp.clip(jax.random.normal(cache_key, (GLOBAL_STREAMS, LEN, KVH * HEAD), jnp.float32), -5.0, 5.0)
    return (query_part, cache_part)


def draw_attention_probes(key, part):
    return drawn_fields(key)[0].astype(jnp.bfloat16)


def draw_stored_attention_lookups(key, part):
    return drawn_fields(key)[1].astype(jnp.bfloat16)


def draw_filled_slot_spans(key, part):
    values = jax.random.randint(jax.random.fold_in(key, 21), (GLOBAL_STREAMS,), 2, LEN + 1)
    return values.at[0].set(LEN).astype(jnp.int32)


def draw_swap_indicator(key, part):
    first_half = jax.random.randint(jax.random.fold_in(key, 31), (SPECIALIST_NUM // 2,), 0, 2)
    first_half = first_half.at[0].set(1).at[1].set(0)
    return jnp.concatenate([first_half, first_half]).astype(jnp.int32)


def touch_ends(result, key, low, high):
    spot = [jax.random.randint(jax.random.fold_in(key, axis), (), 0, length) for axis, length in enumerate(result.shape)]
    longest = result.shape.index(max(result.shape))
    next_to = spot[:longest] + [(spot[longest] + 1) % result.shape[longest]] + spot[longest + 1:]
    return result.at[tuple(spot)].set(low).at[tuple(next_to)].set(high)


def level_of(stream_key, shape, shards, smallest, top_value):
    level = 1.0
    for axis_at, blocks in shards:
        draws = jax.random.uniform(jax.random.fold_in(jax.random.fold_in(stream_key, 6), axis_at), (blocks,), jnp.float32, smallest / len(shards), top_value / len(shards))
        level = level * jnp.repeat(jnp.exp(draws), shape[axis_at] // blocks).reshape((-1,) + (1,) * (len(shape) - 1 - axis_at))
    return level


def shared_out(key, own, number, rows, count, top, bound, slope):
    sequence = jax.random.permutation(key, count)
    heavy_load, ordinary = load_shares(count, rows * top, bound, slope, True), load_shares(count, rows * top, bound, slope, False)
    places = jnp.arange(count)

    def named(lengths, turn):
        used = int((lengths > 0).sum())
        fixed = max(1, used // 4)
        moved = fixed + (places - fixed + turn * (used - fixed)) % max(1, count - fixed)
        return jnp.zeros((count,), jnp.int32).at[sequence[jnp.where(places < fixed, places, moved)]].set(jnp.asarray(lengths, jnp.int32))

    lengths = jnp.where(number % 4 == 0, named(heavy_load, number // 4), named(ordinary, number - number // 4 - 1))
    mixed = jax.random.permutation(jax.random.fold_in(own, 3), count)
    source_of, sink = mixed[0:count // 2 * 2:2], mixed[1:count // 2 * 2:2]
    room = jnp.minimum(lengths[source_of] - 1, bound - lengths[sink]) // 2
    room = jnp.where((source_of == sequence[0]) | (sink == sequence[0]) | (lengths[sink] == 0), 0, jnp.maximum(room, 0))
    moved = jax.random.randint(jax.random.fold_in(own, 4), (count // 2,), 0, 1 << 20) % (room + 1)
    lengths = lengths.at[source_of].add(-moved).at[sink].add(moved)
    labels = jnp.searchsorted(jnp.cumsum(lengths), jnp.arange(rows * top), side="right").astype(jnp.int32)
    table = labels.reshape(top, rows).T
    table = table[jax.random.permutation(jax.random.fold_in(own, 1), rows)]
    turn = jax.random.randint(jax.random.fold_in(own, 2), (rows, 1), 0, top)
    return jnp.take_along_axis(table, (jnp.arange(top)[None, :] + turn) % top, axis=1)


def load_shares(count, total, limit, lean, full):
    portions = [(1 << 20) // math.isqrt(grade ** lean) + 1 for grade in range(1, count + 1)]
    largest = limit if full else min(limit, max(-(-total // count), total * portions[0] // sum(portions)))
    least = 1 if total - largest >= count - 1 else 0
    holding, surplus = [largest] + [least] * (count - 1), total - largest - least * (count - 1)
    while surplus > 0:
        free = [i for i in range(1, count) if holding[i] < largest] or [i for i in range(1, count) if holding[i] < limit]
        pool, remaining = sum([portions[i] for i in free]), surplus
        for i in free:
            addition = min(limit - holding[i], max(1, remaining * portions[i] // pool), surplus)
            holding[i] = holding[i] + addition
            surplus = surplus - addition
    return np.array(holding)


def noise(own_key, extent, deviation, limit, pieces=(), held_as=jnp.bfloat16):
    result = jax.random.normal(own_key, extent, jnp.float32) * deviation
    if len(pieces) > 0:
        result = level_of(own_key, extent, pieces, -0.22, 0.18) * result
    return jnp.clip(result, min=-limit, max=limit).astype(held_as)


def setup_inputs(seed: int = 0) -> dict:
    key_of = jax.random.split(jax.random.key(seed), 16)
    skip_stream = noise(key_of[0], (GLOBAL_STREAMS, D), 1.0, 6.0, ((0, 32),))
    attention_probes = draw_attention_probes(jax.random.fold_in(key_of[15], 71), 0)
    stored_attention_lookups = draw_stored_attention_lookups(jax.random.fold_in(key_of[15], 71), 0)
    stored_attention_contents = noise(key_of[3], (GLOBAL_STREAMS, LEN, KVH * HEAD), 1.0, 6.0, ((0, 32),))
    incoming_lookup_entries = noise(key_of[4], (GLOBAL_STREAMS, KVH * HEAD), 1.0, 6.0, ((0, 32),))
    incoming_content_entries = noise(key_of[5], (GLOBAL_STREAMS, KVH * HEAD), 1.0, 6.0, ((0, 32),))
    filled_slot_spans = draw_filled_slot_spans(jax.random.fold_in(key_of[15], 71), 0)
    layernorm_gain = jnp.clip(1.0 + 0.18 * jax.random.normal(key_of[7], (D,), jnp.float32), 0.1, 1.9)
    routed_specialist_indices_keys = jax.random.split(jax.random.fold_in(key_of[8], 1), GLOBAL_STREAMS // LOCAL_STREAMS)
    routed_specialist_indices_turns = jax.random.permutation(jax.random.fold_in(key_of[8], 3), GLOBAL_STREAMS // LOCAL_STREAMS)
    routed_specialist_indices = jax.vmap(lambda own, number: shared_out(jax.random.fold_in(key_of[8], 2), own, number, LOCAL_STREAMS, SPECIALIST_NUM, ROUTED_PER_TOKEN, CAP, 2))(routed_specialist_indices_keys, routed_specialist_indices_turns).reshape((GLOBAL_STREAMS, ROUTED_PER_TOKEN))
    routing_probabilities = jnp.clip(0.05 + 0.95 * jax.random.uniform(key_of[9], (GLOBAL_STREAMS, ROUTED_PER_TOKEN), jnp.float32) ** level_of(key_of[9], (GLOBAL_STREAMS, ROUTED_PER_TOKEN), ((0, 32),), -0.2, 0.2), 0.05, 1.0)
    admission_limits = touch_ends(jax.random.randint(key_of[10], (SPECIALIST_NUM,), LOCAL_STREAMS * DEVICES * ROUTED_PER_TOKEN // (2 * SPECIALIST_NUM), 2 * LOCAL_STREAMS * DEVICES * ROUTED_PER_TOKEN // SPECIALIST_NUM + 1), jax.random.fold_in(key_of[10], 1), LOCAL_STREAMS * DEVICES * ROUTED_PER_TOKEN // (2 * SPECIALIST_NUM), (2 * LOCAL_STREAMS * DEVICES * ROUTED_PER_TOKEN // SPECIALIST_NUM + 1) - 1).astype(jnp.int32)
    swap_indicator = draw_swap_indicator(jax.random.fold_in(key_of[15], 71), 0)
    gating_projection_matrix = noise(key_of[12], (SPECIALIST_NUM, EXPERT_FF, D), D ** -0.5, 0.09375, ((0, 16), (1, 2)))
    widening_projection_matrix = noise(key_of[13], (SPECIALIST_NUM, EXPERT_FF, D), D ** -0.5, 0.09375, ((0, 16), (1, 2)))
    output_projection_matrix = noise(key_of[14], (SPECIALIST_NUM, EXPERT_FF, D), EXPERT_FF ** -0.5, 0.21875, ((0, 16), (2, 2)))
    return {"skip_stream": skip_stream, "attention_probes": attention_probes, "stored_attention_lookups": stored_attention_lookups, "stored_attention_contents": stored_attention_contents, "incoming_lookup_entries": incoming_lookup_entries, "incoming_content_entries": incoming_content_entries, "filled_slot_spans": filled_slot_spans, "layernorm_gain": layernorm_gain, "routed_specialist_indices": routed_specialist_indices, "routing_probabilities": routing_probabilities, "admission_limits": admission_limits, "swap_indicator": swap_indicator, "gating_projection_matrix": gating_projection_matrix, "widening_projection_matrix": widening_projection_matrix, "output_projection_matrix": output_projection_matrix}


def attention(parts):
    query_rows, key_rows, value_rows, new_key, new_value, valid_len = parts
    seq_count = query_rows.shape[0]
    cache_len = key_rows.shape[1]
    group = QH // KVH
    scale = HEAD ** (-0.5)
    query_view = query_rows.astype(jnp.float32).reshape(seq_count, KVH, group, HEAD)
    key_view = key_rows.astype(jnp.float32).reshape(seq_count, cache_len, KVH, HEAD)
    value_view = value_rows.astype(jnp.float32).reshape(seq_count, cache_len, KVH, HEAD)
    scores = jnp.einsum('skgd,slkd->skgl', query_view, key_view) * scale
    valid = jnp.arange(cache_len, dtype=jnp.int32)[None, :] < valid_len[:, None]
    scores = jnp.where(valid[:, None, None, :], scores, -1e+30)
    own_score = jnp.einsum('skgd,skd->skg', query_view, new_key.astype(jnp.float32).reshape(seq_count, KVH, HEAD)) * scale
    highest = jnp.maximum(lax.optimization_barrier(jnp.max(scores, axis=-1)), own_score)
    weights = jnp.exp(scores - highest[..., None])
    own_weight = jnp.exp(own_score - highest)
    denom = lax.optimization_barrier(jnp.sum(weights, axis=-1)) + own_weight
    probs = (weights / denom[..., None]).astype(jnp.bfloat16)
    own_prob = (own_weight / denom).astype(jnp.bfloat16)
    mixed = jnp.einsum('skgl,slkd->skgd', probs.astype(jnp.float32), value_view)
    mixed = mixed + own_prob.astype(jnp.float32)[..., None] * new_value.astype(jnp.float32).reshape(seq_count, KVH, 1, HEAD)
    return mixed.reshape(seq_count, QH * HEAD).astype(jnp.bfloat16)

def reference(skip_stream, attention_probes, stored_attention_lookups, stored_attention_contents, incoming_lookup_entries, incoming_content_entries, filled_slot_spans, layernorm_gain, routed_specialist_indices, routing_probabilities, admission_limits, swap_indicator, gating_projection_matrix, widening_projection_matrix, output_projection_matrix):
    blocks = GLOBAL_STREAMS // LOCAL_STREAMS
    attn = lax.map(attention, (attention_probes.reshape(blocks, LOCAL_STREAMS, D), stored_attention_lookups.reshape(blocks, LOCAL_STREAMS, LEN, KVH * HEAD), stored_attention_contents.reshape(blocks, LOCAL_STREAMS, LEN, KVH * HEAD), incoming_lookup_entries.reshape(blocks, LOCAL_STREAMS, KVH * HEAD), incoming_content_entries.reshape(blocks, LOCAL_STREAMS, KVH * HEAD), filled_slot_spans.reshape(blocks, LOCAL_STREAMS)))
    attn = attn.reshape(GLOBAL_STREAMS, D)
    stream = skip_stream.astype(jnp.float32) + attn.astype(jnp.float32)
    normed = (stream * lax.rsqrt(lax.optimization_barrier(jnp.mean(stream * stream, axis=-1, keepdims=True)) + 1e-06) * layernorm_gain).astype(jnp.bfloat16)
    expert_range = jnp.arange(SPECIALIST_NUM, dtype=jnp.int32)
    route_hot = (routed_specialist_indices[:, :, None] == expert_range[None, None, :]).astype(jnp.int32)
    row_hot = lax.optimization_barrier(jnp.sum(route_hot, axis=1))
    earlier = jnp.cumsum(row_hot, axis=0) - row_hot
    pair_rank = lax.optimization_barrier(jnp.sum(route_hot * earlier[:, None, :], axis=-1)).astype(jnp.int32)
    specialist_tallies = lax.optimization_barrier(jnp.sum(row_hot, axis=0))
    paired_limit = jnp.take(admission_limits, routed_specialist_indices)
    kept = pair_rank < paired_limit
    slot_bound = 2 * GLOBAL_STREAMS * ROUTED_PER_TOKEN // SPECIALIST_NUM
    row_index = jnp.repeat(jnp.arange(GLOBAL_STREAMS, dtype=jnp.int32), ROUTED_PER_TOKEN)
    source_rows = jnp.full((SPECIALIST_NUM, slot_bound), GLOBAL_STREAMS, jnp.int32).at[routed_specialist_indices.reshape(-1), pair_rank.reshape(-1)].set(row_index, mode='drop')
    normed_pad = jnp.concatenate([normed, jnp.zeros((1, D), jnp.bfloat16)], axis=0)

    def expert_rows(parts):
        picks, gate_mat, up_mat, down_mat = parts
        rows_in = normed_pad[picks]
        gate_val = jnp.dot(rows_in, gate_mat.T, preferred_element_type=jnp.float32)
        up_val = jnp.dot(rows_in, up_mat.T, preferred_element_type=jnp.float32)
        hidden_val = (jax.nn.silu(gate_val) * up_val).astype(jnp.bfloat16)
        return jnp.dot(hidden_val, down_mat, preferred_element_type=jnp.float32).astype(jnp.bfloat16)
    outputs = lax.map(expert_rows, (source_rows, gating_projection_matrix, widening_projection_matrix, output_projection_matrix))
    expert_mix = jnp.zeros((GLOBAL_STREAMS, D), jnp.float32)
    for choice_k in range(ROUTED_PER_TOKEN):
        picked = outputs[routed_specialist_indices[:, choice_k], jnp.minimum(pair_rank[:, choice_k], slot_bound - 1)]
        factor = jnp.where(kept[:, choice_k], routing_probabilities[:, choice_k], 0.0)
        expert_mix = expert_mix + factor[:, None] * picked.astype(jnp.float32)
    layer_out = (stream + expert_mix).astype(jnp.bfloat16)
    retained_specialist = jnp.where(swap_indicator == 1, (expert_range + SPECIALIST_NUM // 2) % SPECIALIST_NUM, expert_range).astype(jnp.int32)
    held_gate = jnp.take(gating_projection_matrix, retained_specialist, axis=0)
    held_up = jnp.take(widening_projection_matrix, retained_specialist, axis=0)
    held_down = jnp.take(output_projection_matrix, retained_specialist, axis=0)
    handled_specialist = jnp.minimum(specialist_tallies, admission_limits).astype(jnp.float32) / (GLOBAL_STREAMS * ROUTED_PER_TOKEN / SPECIALIST_NUM)
    device_share = jnp.take(handled_specialist, retained_specialist)
    return (layer_out, device_share, held_gate, held_up, held_down)
```

```python
import itertools

import jax
import jax.numpy as jnp
import numpy as np
from jax import lax
from jax.sharding import PartitionSpec as P

QH = 32
KVH = 4
HEAD = 128


SWITCHED_PAIRS = 8


def pair_lines():
    return [[j for j in range(SWITCHED_PAIRS) if (j >> 1) & 1 == x] for x in range(2)]


def branch_table():
    lines = pair_lines()
    sets = []
    for count in range(len(lines[0]) + 1):
        for first in itertools.combinations(lines[0], count):
            for second in itertools.combinations(lines[1], count):
                sets.append(sum(1 << j for j in first + second))
    table = [
        next(k for k, members in enumerate(sets) if members & pattern == pattern)
        for pattern in range(2**SWITCHED_PAIRS)
    ]
    return sets, np.array(table, np.int32)


def moved_weights(weights, swap_indicator, experts):
    half_axis = experts // 2

    def exchange(members):
        def move(operands):
            pairs = [
                (i, (i + half_axis) % experts)
                for i in range(experts)
                if (members >> (i % half_axis)) & 1
            ]
            return tuple(lax.ppermute(own, "expert", pairs) for own in operands)

        return move if members else lambda operands: operands

    if half_axis == SWITCHED_PAIRS:
        sets, table = branch_table()
        bits = swap_indicator[:half_axis] << lax.broadcasted_iota(jnp.int32, (half_axis,), 0)
        choice = jnp.asarray(table)[jnp.sum(bits)]
        partner = lax.switch(choice, [exchange(members) for members in sets], weights)
    else:
        partner = exchange(2**half_axis - 1)(weights)
    take_other = swap_indicator[lax.axis_index("expert")] == 1
    return tuple(jnp.where(take_other, far, own) for far, own in zip(partner, weights))


def attention(query_rows, key_rows, value_rows, new_key, new_value, valid_len):
    seq_count = query_rows.shape[0]
    cache_len = key_rows.shape[1]
    group = QH // KVH
    scale = HEAD ** (-0.5)
    query_view = query_rows.reshape(seq_count, KVH, group, HEAD)
    key_view = key_rows.reshape(seq_count, cache_len, KVH, HEAD)
    value_view = value_rows.reshape(seq_count, cache_len, KVH, HEAD)
    scores = (
        jnp.einsum("skgd,slkd->skgl", query_view, key_view, preferred_element_type=jnp.float32)
        * scale
    )
    valid = lax.broadcasted_iota(jnp.int32, (seq_count, cache_len), 1) < valid_len[:, None]
    scores = jnp.where(valid[:, None, None, :], scores, -1e30)
    own_score = (
        jnp.einsum(
            "skgd,skd->skg",
            query_view,
            new_key.reshape(seq_count, KVH, HEAD),
            preferred_element_type=jnp.float32,
        )
        * scale
    )
    highest = jnp.maximum(jnp.max(scores, axis=-1), own_score)
    weights = jnp.exp(scores - highest[..., None])
    own_weight = jnp.exp(own_score - highest)
    denom = jnp.sum(weights, axis=-1) + own_weight
    probs = (weights / denom[..., None]).astype(jnp.bfloat16)
    own_prob = (own_weight / denom).astype(jnp.bfloat16)
    mixed = jnp.einsum("skgl,slkd->skgd", probs, value_view, preferred_element_type=jnp.float32)
    mixed = mixed + own_prob.astype(jnp.float32)[..., None] * new_value.reshape(
        seq_count, KVH, 1, HEAD
    ).astype(jnp.float32)
    return mixed.reshape(seq_count, QH * HEAD).astype(jnp.bfloat16)


def per_device(
    skip_stream,
    attention_probes,
    stored_attention_lookups,
    stored_attention_contents,
    incoming_lookup_entries,
    incoming_content_entries,
    filled_slot_spans,
    layernorm_gain,
    routed_specialist_indices,
    routing_probabilities,
    admission_limits,
    swap_indicator,
    gating_projection_matrix,
    widening_projection_matrix,
    output_projection_matrix,
):
    experts = lax.axis_size("expert")
    groups = lax.axis_size("dp")
    half_axis = experts // 2
    my_index = lax.axis_index("expert")
    my_block = my_index * groups + lax.axis_index("dp")
    gate_own = gating_projection_matrix[0]
    up_own = widening_projection_matrix[0]
    down_own = output_projection_matrix[0]
    seq_rows, top_count = routed_specialist_indices.shape
    width = skip_stream.shape[1]
    feature_cols = down_own.shape[1]
    slot_cap = max(2, (seq_rows * top_count + experts - 1) // experts)
    all_routes = lax.all_gather(routed_specialist_indices, ("expert", "dp"), axis=0, tiled=True)
    attn = attention(
        attention_probes,
        stored_attention_lookups,
        stored_attention_contents,
        incoming_lookup_entries,
        incoming_content_entries,
        filled_slot_spans,
    )
    stream = skip_stream.astype(jnp.float32) + attn.astype(jnp.float32)
    normed = (
        stream
        * lax.rsqrt(jnp.mean(stream * stream, axis=-1, keepdims=True) + 1e-06)
        * layernorm_gain
    ).astype(jnp.bfloat16)
    expert_range = lax.broadcasted_iota(jnp.int32, (experts,), 0)
    route_hot = routed_specialist_indices[:, :, None] == expert_range[None, None, :]
    row_hot = jnp.any(route_hot, axis=1).astype(jnp.int32)
    row_order = lax.broadcasted_iota(jnp.int32, (seq_rows, seq_rows), 0)
    earlier_row = lax.broadcasted_iota(jnp.int32, (seq_rows, seq_rows), 1)
    local_rank = jnp.sum(
        jnp.where((earlier_row < row_order)[:, :, None], row_hot[None, :, :], 0), axis=1
    )
    slots = lax.broadcasted_iota(jnp.int32, (seq_rows, experts, slot_cap), 2)
    place = (row_hot[:, :, None] == 1) & (local_rank[:, :, None] == slots)
    outgoing = jnp.einsum(
        "set,sf->etf",
        place.astype(jnp.bfloat16),
        normed,
        preferred_element_type=jnp.float32,
    ).astype(jnp.bfloat16)
    outgoing = jnp.broadcast_to(outgoing[:, None], (experts, groups, slot_cap, width))
    arrived = lax.all_to_all(
        outgoing.reshape(experts * groups, slot_cap, width),
        ("expert", "dp"),
        split_axis=0,
        concat_axis=0,
        tiled=True,
    )
    blocks = experts * groups
    rows_in = arrived.reshape(blocks * slot_cap, width)
    gate_val = jnp.einsum("sf,hf->sh", rows_in, gate_own, preferred_element_type=jnp.float32)
    up_val = jnp.einsum("sf,hf->sh", rows_in, up_own, preferred_element_type=jnp.float32)
    hidden = (jax.nn.silu(gate_val) * up_val).astype(jnp.bfloat16)
    hidden_all = lax.all_gather(hidden, "dp", axis=1, tiled=True)
    results = jnp.dot(hidden_all, down_own, preferred_element_type=jnp.float32)
    returned = lax.all_to_all(
        results.astype(jnp.bfloat16).reshape(blocks, slot_cap, feature_cols),
        ("expert", "dp"),
        split_axis=0,
        concat_axis=0,
        tiled=True,
    ).reshape(experts, groups, slot_cap, feature_cols)
    named = jnp.any(all_routes[:, :, None] == expert_range[None, None, :], axis=1)
    named = named.astype(jnp.int32)
    before = lax.broadcasted_iota(jnp.int32, (named.shape[0], 1), 0) < my_block * seq_rows
    rank = local_rank + jnp.sum(jnp.where(before, named, 0), axis=0)[None, :]
    kept = rank < admission_limits[None, :]
    weight = jnp.sum(jnp.where(route_hot, routing_probabilities[:, :, None], 0.0), axis=1)
    factor = jnp.where(kept, weight, 0.0)
    mix = jnp.where(place, factor[:, :, None], 0.0)
    expert_mix = jnp.einsum(
        "set,edtf->sdf",
        mix,
        returned.astype(jnp.float32),
        precision=lax.Precision.HIGHEST,
        preferred_element_type=jnp.float32,
    ).reshape(seq_rows, width)
    layer_out = (stream + expert_mix).astype(jnp.bfloat16)
    mean_load = named.shape[0] * top_count / experts
    served = jnp.minimum(jnp.sum(named, axis=0), admission_limits).astype(jnp.float32) / mean_load
    take_other = swap_indicator[my_index] == 1
    retained = jnp.where(take_other, (my_index + half_axis) % experts, my_index)
    device_share = jnp.sum(jnp.where(expert_range == retained, served, 0.0))
    gate_held, up_held, down_held = moved_weights(
        (gate_own, up_own, down_own), swap_indicator, experts
    )
    return (layer_out, device_share.reshape(1), gate_held[None], up_held[None], down_held[None])


def solution(mesh):
    in_specs = (
        P(("expert", "dp"), None),
        P(("expert", "dp"), None),
        P(("expert", "dp"), None, None),
        P(("expert", "dp"), None, None),
        P(("expert", "dp"), None),
        P(("expert", "dp"), None),
        P(("expert", "dp")),
        P(),
        P(("expert", "dp"), None),
        P(("expert", "dp"), None),
        P(),
        P(),
        P("expert", "dp", None),
        P("expert", "dp", None),
        P("expert", None, "dp"),
    )
    out_specs = (
        P(("expert", "dp"), None),
        P("expert"),
        P("expert", "dp", None),
        P("expert", "dp", None),
        P("expert", None, "dp"),
    )
    return jax.shard_map(
        per_device, mesh=mesh, in_specs=in_specs, out_specs=out_specs, check_vma=False
    )
```

```python
import itertools

import jax
import jax.numpy as jnp
import numpy as np
from jax import lax
from jax.sharding import PartitionSpec as P

QH = 32
KVH = 4
HEAD = 128


SWITCHED_PAIRS = 8


def pair_lines():
    return [[j for j in range(SWITCHED_PAIRS) if (j >> 1) & 1 == x] for x in range(2)]


def branch_table():
    lines = pair_lines()
    sets = []
    for count in range(len(lines[0]) + 1):
        for first in itertools.combinations(lines[0], count):
            for second in itertools.combinations(lines[1], count):
                sets.append(sum(1 << j for j in first + second))
    table = [
        next(k for k, members in enumerate(sets) if members & pattern == pattern)
        for pattern in range(2**SWITCHED_PAIRS)
    ]
    return sets, np.array(table, np.int32)


def moved_weights(weights, swap_indicator, experts):
    half_axis = experts // 2

    def exchange(members):
        def move(operands):
            pairs = [
                (i, (i + half_axis) % experts)
                for i in range(experts)
                if (members >> (i % half_axis)) & 1
            ]
            return tuple(lax.ppermute(own, "expert", pairs) for own in operands)

        return move if members else lambda operands: operands

    if half_axis == SWITCHED_PAIRS:
        sets, table = branch_table()
        bits = swap_indicator[:half_axis] << lax.broadcasted_iota(jnp.int32, (half_axis,), 0)
        choice = jnp.asarray(table)[jnp.sum(bits)]
        partner = lax.switch(choice, [exchange(members) for members in sets], weights)
    else:
        partner = exchange(2**half_axis - 1)(weights)
    take_other = swap_indicator[lax.axis_index("expert")] == 1
    return tuple(jnp.where(take_other, far, own) for far, own in zip(partner, weights))


def attention(query_rows, key_rows, value_rows, new_key, new_value, valid_len):
    seq_count = query_rows.shape[0]
    cache_len = key_rows.shape[1]
    group = QH // KVH
    scale = HEAD ** (-0.5)
    query_view = query_rows.reshape(seq_count, KVH, group, HEAD)
    key_view = key_rows.reshape(seq_count, cache_len, KVH, HEAD)
    value_view = value_rows.reshape(seq_count, cache_len, KVH, HEAD)
    scores = (
        jnp.einsum("skgd,slkd->skgl", query_view, key_view, preferred_element_type=jnp.float32)
        * scale
    )
    valid = lax.broadcasted_iota(jnp.int32, (seq_count, cache_len), 1) < valid_len[:, None]
    scores = jnp.where(valid[:, None, None, :], scores, -1e30)
    own_score = (
        jnp.einsum(
            "skgd,skd->skg",
            query_view,
            new_key.reshape(seq_count, KVH, HEAD),
            preferred_element_type=jnp.float32,
        )
        * scale
    )
    highest = jnp.maximum(jnp.max(scores, axis=-1), own_score)
    weights = jnp.exp(scores - highest[..., None])
    own_weight = jnp.exp(own_score - highest)
    denom = jnp.sum(weights, axis=-1) + own_weight
    probs = (weights / denom[..., None]).astype(jnp.bfloat16)
    own_prob = (own_weight / denom).astype(jnp.bfloat16)
    mixed = jnp.einsum("skgl,slkd->skgd", probs, value_view, preferred_element_type=jnp.float32)
    mixed = mixed + own_prob.astype(jnp.float32)[..., None] * new_value.reshape(
        seq_count, KVH, 1, HEAD
    ).astype(jnp.float32)
    return mixed.reshape(seq_count, QH * HEAD).astype(jnp.bfloat16)


def per_device(
    skip_stream,
    attention_probes,
    stored_attention_lookups,
    stored_attention_contents,
    incoming_lookup_entries,
    incoming_content_entries,
    filled_slot_spans,
    layernorm_gain,
    routed_specialist_indices,
    routing_probabilities,
    admission_limits,
    swap_indicator,
    gating_projection_matrix,
    widening_projection_matrix,
    output_projection_matrix,
):
    experts = lax.axis_size("expert")
    groups = lax.axis_size("dp")
    half_axis = experts // 2
    my_index = lax.axis_index("expert")
    my_block = my_index * groups + lax.axis_index("dp")
    gate_own = gating_projection_matrix[0]
    up_own = widening_projection_matrix[0]
    down_own = output_projection_matrix[0]
    seq_rows, top_count = routed_specialist_indices.shape
    width = skip_stream.shape[1]
    feature_cols = down_own.shape[1]
    slot_cap = max(2, (seq_rows * top_count + experts - 1) // experts)
    attn = attention(
        attention_probes,
        stored_attention_lookups,
        stored_attention_contents,
        incoming_lookup_entries,
        incoming_content_entries,
        filled_slot_spans,
    )
    stream = skip_stream.astype(jnp.float32) + attn.astype(jnp.float32)
    normed = (
        stream
        * lax.rsqrt(jnp.mean(stream * stream, axis=-1, keepdims=True) + 1e-06)
        * layernorm_gain
    ).astype(jnp.bfloat16)
    expert_range = lax.broadcasted_iota(jnp.int32, (experts,), 0)
    route_hot = routed_specialist_indices[:, :, None] == expert_range[None, None, :]
    row_hot = jnp.any(route_hot, axis=1).astype(jnp.int32)
    row_order = lax.broadcasted_iota(jnp.int32, (seq_rows, seq_rows), 0)
    earlier_row = lax.broadcasted_iota(jnp.int32, (seq_rows, seq_rows), 1)
    local_rank = jnp.sum(
        jnp.where((earlier_row < row_order)[:, :, None], row_hot[None, :, :], 0), axis=1
    )
    slots = lax.broadcasted_iota(jnp.int32, (seq_rows, experts, slot_cap), 2)
    place = (row_hot[:, :, None] == 1) & (local_rank[:, :, None] == slots)
    outgoing = jnp.einsum(
        "set,sf->etf",
        place.astype(jnp.bfloat16),
        normed,
        preferred_element_type=jnp.float32,
    ).astype(jnp.bfloat16)
    blocks = experts * groups
    side = -(-experts // 128) * 128
    counts_out = jnp.pad(jnp.sum(row_hot, axis=0), (0, side - experts)).astype(jnp.bfloat16)
    counts_out = jnp.broadcast_to(counts_out, (experts, slot_cap, side))
    outgoing = jnp.concatenate([outgoing, counts_out], axis=-1)
    outgoing = jnp.broadcast_to(outgoing[:, None], (experts, groups, slot_cap, width + side))
    arrived = lax.all_to_all(
        outgoing.reshape(blocks, slot_cap, width + side),
        ("expert", "dp"),
        split_axis=0,
        concat_axis=0,
        tiled=True,
    )
    rows_in = arrived[:, :, :width].reshape(blocks * slot_cap, width)
    gate_val = jnp.einsum("sf,hf->sh", rows_in, gate_own, preferred_element_type=jnp.float32)
    up_val = jnp.einsum("sf,hf->sh", rows_in, up_own, preferred_element_type=jnp.float32)
    hidden = (jax.nn.silu(gate_val) * up_val).astype(jnp.bfloat16)
    hidden_all = lax.all_gather(hidden, "dp", axis=1, tiled=True)
    results = jnp.dot(hidden_all, down_own, preferred_element_type=jnp.float32)
    returned = lax.all_to_all(
        results.astype(jnp.bfloat16).reshape(blocks, slot_cap, feature_cols),
        ("expert", "dp"),
        split_axis=0,
        concat_axis=0,
        tiled=True,
    ).reshape(experts, groups, slot_cap, feature_cols)
    counts = arrived[:, 0, width : width + experts].astype(jnp.int32)
    before = lax.broadcasted_iota(jnp.int32, (blocks, 1), 0) < my_block
    rank = local_rank + jnp.sum(jnp.where(before, counts, 0), axis=0)[None, :]
    kept = rank < admission_limits[None, :]
    weight = jnp.sum(jnp.where(route_hot, routing_probabilities[:, :, None], 0.0), axis=1)
    factor = jnp.where(kept, weight, 0.0)
    mix = jnp.where(place, factor[:, :, None], 0.0)
    expert_mix = jnp.einsum(
        "set,edtf->sdf",
        mix,
        returned.astype(jnp.float32),
        precision=lax.Precision.HIGHEST,
        preferred_element_type=jnp.float32,
    ).reshape(seq_rows, width)
    layer_out = (stream + expert_mix).astype(jnp.bfloat16)
    mean_load = blocks * seq_rows * top_count / experts
    served = jnp.minimum(jnp.sum(counts, axis=0), admission_limits).astype(jnp.float32) / mean_load
    take_other = swap_indicator[my_index] == 1
    retained = jnp.where(take_other, (my_index + half_axis) % experts, my_index)
    device_share = jnp.sum(jnp.where(expert_range == retained, served, 0.0))
    gate_held, up_held, down_held = moved_weights(
        (gate_own, up_own, down_own), swap_indicator, experts
    )
    return (layer_out, device_share.reshape(1), gate_held[None], up_held[None], down_held[None])


def solution(mesh):
    in_specs = (
        P(("expert", "dp"), None),
        P(("expert", "dp"), None),
        P(("expert", "dp"), None, None),
        P(("expert", "dp"), None, None),
        P(("expert", "dp"), None),
        P(("expert", "dp"), None),
        P(("expert", "dp")),
        P(),
        P(("expert", "dp"), None),
        P(("expert", "dp"), None),
        P(),
        P(),
        P("expert", "dp", None),
        P("expert", "dp", None),
        P("expert", None, "dp"),
    )
    out_specs = (
        P(("expert", "dp"), None),
        P("expert"),
        P("expert", "dp", None),
        P("expert", "dp", None),
        P("expert", None, "dp"),
    )
    return jax.shard_map(
        per_device, mesh=mesh, in_specs=in_specs, out_specs=out_specs, check_vma=False
    )
```
